32 devices in a mesh: row: 8 (over z, core), col: 4 (over y, x).
Axes of the slice: x: 2, y: 2, z: 4, core: 2. Of those that a mesh axis runs over, the one named last changes fastest.
Arguments:
- features: bfloat16 [192, 96, 256], P('row', 'col'), may hold values from -6 to 6
- kernels: bfloat16 [4608, 128], P('row', 'col'), may hold values from -0.125 to 0.125
- out_cotangent: bfloat16 [2, 192, 96, 128], P(None, 'row', 'col'), may hold values from -6 to 6
Outputs:
- branch_maps: bfloat16 [2, 192, 96, 128], P(None, 'row', 'col')
- input_grad: bfloat16 [192, 96, 256], P('row', 'col')
- kernel_grad: float32 [4608, 128], P('row', 'col')
The draws below stay inside these ranges and needn't reach their ends.
All inputs are finite; a program needn't handle non-finite values.
Results may differ from the reference program's by a relative error of at most 0.001.
Values may be sent and summed in bfloat16 or wider, within the bound.
A program may use at most 64 MiB of HBM per device.

```python
import jax
import jax.numpy as jnp

C = 256
COUT = 128
FIRST_SPACING = 12
SECOND_SPACING = 24
NH = 192
NW = 96


def shard_levels(rng, dims, shards, low, high):
    gain, own = 1.0, jax.random.fold_in(rng, 6)
    for dim, shards_of in shards:
        heights = jnp.exp(jax.random.uniform(jax.random.fold_in(own, dim), (shards_of,), jnp.float32, low / len(shards), high / len(shards)))
        gain = gain * jnp.repeat(heights, dims[dim] // shards_of).reshape([-1 if axis == dim else 1 for axis in range(len(dims))])
    return gain


def bell_draw(stream_key, extent, deviation, limit, shards=(), held_as=jnp.bfloat16):
    result = deviation * jax.random.normal(stream_key, extent, jnp.float32)
    if shards:
        result = result * shard_levels(stream_key, extent, shards, -0.22, 0.18)
    return jnp.clip(result, -limit, limit).astype(held_as)


def setup_inputs(seed: int = 0) -> dict:
    streams_of = jax.random.split(jax.random.key(seed), 4)
    features = bell_draw(streams_of[0], (NH, NW, C), 1.0, 6.0, ((0, 8), (1, 4)))
    kernels = bell_draw(streams_of[1], (18 * C, COUT), (9 * C) ** -0.5, 0.125, ((0, 8), (1, 4)))
    out_cotangent = bell_draw(streams_of[2], (2, NH, NW, COUT), 1.0, 6.0, ((1, 8), (2, 4)))
    return {"features": features, "kernels": kernels, "out_cotangent": out_cotangent}


def reference(features, kernels, out_cotangent):
    padding_margin = SECOND_SPACING
    x_pad = jnp.pad(features, ((padding_margin, padding_margin), (padding_margin, padding_margin), (0, 0)))
    g_pad = jnp.pad(out_cotangent, ((0, 0), (padding_margin, padding_margin), (padding_margin, padding_margin), (0, 0)))
    blocks = kernels.reshape(2, 9, C, COUT)
    maps = []
    grad_in = jnp.zeros((NH * NW, C), jnp.float32)
    grads = []
    scale = 1.0 / jnp.sqrt(jnp.float32(NH * NW))
    for branch_index, dilation_rate in ((0, FIRST_SPACING), (1, SECOND_SPACING)):
        acc = jnp.zeros((NH * NW, COUT), jnp.float32)
        g_flat = out_cotangent[branch_index].reshape(NH * NW, COUT)
        for kernel_tap in range(9):
            shift_down = (kernel_tap // 3 - 1) * dilation_rate
            shift_across = (kernel_tap % 3 - 1) * dilation_rate
            x_tap = x_pad[padding_margin + shift_down:padding_margin + shift_down + NH, padding_margin + shift_across:padding_margin + shift_across + NW].reshape(NH * NW, C)
            weight = blocks[branch_index, kernel_tap]
            acc = acc + jnp.dot(x_tap, weight, preferred_element_type=jnp.float32)
            g_tap = g_pad[branch_index, padding_margin - shift_down:padding_margin - shift_down + NH, padding_margin - shift_across:padding_margin - shift_across + NW].reshape(NH * NW, COUT)
            grad_in = grad_in + jnp.dot(g_tap, weight.T, preferred_element_type=jnp.float32)
            grads.append(jnp.dot(x_tap.T, g_flat, preferred_element_type=jnp.float32) * scale)
        maps.append(acc.reshape(NH, NW, COUT).astype(jnp.bfloat16))
    branch_maps = jnp.stack(maps, 0)
    input_grad = grad_in.reshape(NH, NW, C).astype(jnp.bfloat16)
    kernel_grad = jnp.concatenate(grads, 0)
    return (branch_maps, input_grad, kernel_grad)
```

```python
import functools

import jax
import jax.numpy as jnp
from jax import lax
from jax.experimental import pallas as pl
from jax.experimental.pallas import tpu as pltpu
from jax.sharding import PartitionSpec as P

FIRST_SPACING = 12
SECOND_SPACING = 24
UNITS = 36
PIECE = 36
SLOT = 48
MESH = pl.DeviceIdType.MESH


def kernel(n_row, n_col, scale, gs_ref, xs_ref, ks_ref, om_ref, oi_ref, ok_ref,
           ga, xa, gp, xp, kb, k2, ru, ra, sb, rb_, tc, rc, fin, fx, macc, iacc, ms, igs,
           a_send, a_recv, h_send, h_recv, k_send, k_recv, o_send, o_recv, r_send, r_recv):
    nz = n_row // 2
    per_z = UNITS // nz
    r = lax.axis_index("row")
    j = lax.axis_index("col")
    z = r // 2
    c = r % 2
    sib = r + 1 - 2 * c
    cols = [lax.rem(j + i, n_col) for i in range(1, n_col)]
    zs = [lax.rem(z + i, nz) for i in range(1, nz)]
    far = r - 1 + 2 * c
    has_up = r > 0
    has_down = r < n_row - 1
    has_far = jnp.where(c == 0, has_up, has_down)

    barrier = pltpu.get_barrier_semaphore()
    for s in cols:
        pl.semaphore_signal(barrier, inc=1, device_id={"col": s}, device_id_type=MESH)
    for zz in zs:
        pl.semaphore_signal(barrier, inc=1, device_id={"row": zz * 2 + c}, device_id_type=MESH)
    pl.semaphore_signal(barrier, inc=1, device_id={"row": sib}, device_id_type=MESH)

    @pl.when(has_far)
    def _():
        pl.semaphore_signal(barrier, inc=1, device_id={"row": far}, device_id_type=MESH)

    pl.semaphore_wait(barrier, n_col - 1 + nz - 1 + 1 + jnp.where(has_far, 1, 0))

    def remote(src, dst, ssem, rsem, dev):
        return pltpu.make_async_remote_copy(
            src_ref=src, dst_ref=dst, send_sem=ssem, recv_sem=rsem,
            device_id=dev, device_id_type=MESH)

    arrays = ((gs_ref, ga), (xs_ref, xa))
    sends = []
    for a, (src, dst) in enumerate(arrays):
        for s in cols:
            cp = remote(src.at[s], dst.at[1, j], a_send.at[a, s], a_recv.at[a, j], {"col": s})
            cp.start()
            sends.append(cp)
        if a == 0:
            for zz in zs:
                cp = remote(ks_ref, kb.at[c, j, z], k_send.at[0, zz], k_recv.at[0, z], {"row": zz * 2 + c})
                cp.start()
                sends.append(cp)
    kb[c, j, z] = ks_ref[...]
    for src, dst in arrays:
        dst[1, j] = src[j]
    gp[...] = jnp.zeros_like(gp)
    xp[...] = jnp.zeros_like(xp)

    def halo(a, s, up):
        buf = arrays[a][1]
        to = r - 1 if up else r + 1
        d = 0 if up else 1
        return remote(buf.at[1, s], buf.at[2 if up else 0, s],
                      h_send.at[a, d, s], h_recv.at[a, d, s], {"row": to})

    def spread(a, s):
        @pl.when(has_up)
        def _():
            halo(a, s, True).start()

        @pl.when(has_down)
        def _():
            halo(a, s, False).start()

    def gather(a):
        src, dst = arrays[a]
        spread(a, j)
        for i in range(1, n_col):
            s = lax.rem(j + n_col - i, n_col)
            remote(src.at[s], dst.at[1, s], a_send.at[a, s], a_recv.at[a, s], {"col": s}).wait_recv()
            spread(a, s)

    def halo_wait(a):
        for s in range(n_col):
            @pl.when(has_down)
            def _():
                halo(a, s, True).wait_recv()

            @pl.when(has_up)
            def _():
                halo(a, s, False).wait_recv()

    def halo_done(a):
        for s in range(n_col):
            @pl.when(has_up)
            def _():
                halo(a, s, True).wait_send()

            @pl.when(has_down)
            def _():
                halo(a, s, False).wait_send()

    gather(0)
    for i in range(1, nz):
        zz = lax.rem(z + nz - i, nz)
        remote(ks_ref, kb.at[c, j, zz], k_send.at[0, zz], k_recv.at[0, zz], {"row": zz * 2 + c}).wait_recv()
    for s in cols:
        cp = remote(kb.at[c, j], kb.at[c, j], k_send.at[1, s], k_recv.at[1, j], {"col": s})
        cp.start()
        sends.append(cp)
    gather(1)

    def place(n):
        for s in range(n_col):
            for b in range(2):
                block = ga[n, s, b].astype(jnp.float32)
                for m in range(4):
                    part = block[PIECE * m : PIECE * (m + 1)].astype(jnp.bfloat16)
                    gp[b, 2 * n + m // 2, 2 + 2 * s + m % 2, 0:PIECE, :] = part

    def place_x(n):
        for s in range(n_col):
            block = xa[n, s].astype(jnp.float32)
            for m in range(4):
                part = block[PIECE * m : PIECE * (m + 1)].astype(jnp.bfloat16)
                xp[2 * n + m // 2, 2 + 2 * s + m % 2, 0:PIECE, :] = part

    place(1)
    place_x(1)
    halo_wait(0)

    @pl.when(has_up)
    def _():
        place(0)

    @pl.when(has_down)
    def _():
        place(2)

    qs = 2 * n_col
    pix = 2 * qs * SLOT

    def g_tap(b, t):
        d = 1 + b
        sy = (t // 3 - 1) * d
        sx = (t % 3 - 1) * d
        return gp[b, pl.ds(2 - sy, 2), pl.ds(2 - sx, qs)].reshape(pix, gp.shape[-1])

    def x_tap(b, t):
        d = 1 + b
        sy = (t // 3 - 1) * d
        sx = (t % 3 - 1) * d
        return xp[pl.ds(2 + sy, 2), pl.ds(2 + sx, qs)].reshape(pix, xp.shape[-1])

    outs_n = gp.shape[-1]
    per_col = outs_n // n_col
    half = per_col // 2

    def pair(b):
        us = pl.ds(18 * b, 18)
        return remote(ru.at[us, :, 1 - c], ra.at[us], r_send.at[0, b], r_recv.at[0, b], {"row": sib})

    for b in (1, 0):
        def body(t, carry):
            x_here = xp[pl.ds(2, 2), pl.ds(2, qs)].reshape(pix, xp.shape[-1])
            res = lax.dot_general(g_tap(b, t), x_here, (((0,), (0,)), ((), ())),
                                  preferred_element_type=jnp.float32)
            for h in range(2):
                ru[2 * (9 * b + t) + h] = res[:, 128 * h : 128 * (h + 1)].reshape(n_col, 2, half, 128)
            return carry

        lax.fori_loop(0, 9, body, 0)
        pair(b).start()

    for i in range(1, n_col):
        s = lax.rem(j + n_col - i, n_col)
        remote(kb.at[c, s], kb.at[c, s], k_send.at[1, s], k_recv.at[1, s], {"col": s}).wait_recv()
    swap = remote(kb.at[c], kb.at[c], k_send.at[2, 0], k_recv.at[2, 0], {"row": sib})
    swap.start()
    sends.append(swap)

    def plane(b, s):
        us = pl.ds(18 * b, 18)
        return remote(sb.at[s, us], rb_.at[j, us], r_send.at[1 + b, s], r_recv.at[1 + b, j], {"col": s})

    for b in (1, 0):
        us = pl.ds(18 * b, 18)
        pair(b).wait_recv()
        for s in range(n_col):
            sb[s, us] = ru[us, s, c] + ra[us, s]
        for s in cols:
            plane(b, s).start()

    remote(kb.at[1 - c], kb.at[1 - c], k_send.at[2, 0], k_recv.at[2, 0], {"row": sib}).wait_recv()
    for u in range(UNITS):
        zz, v = divmod(u, per_z)
        mid = per_z // 2
        if v < mid:
            val = kb[0, :, zz, v]
        elif v > mid:
            val = kb[1, :, zz, v - mid]
        else:
            val = kb[0, :, zz, mid] + kb[1, :, zz, 0]
        k2[u // 2, :, 128 * (u % 2) : 128 * (u % 2 + 1)] = val.reshape(outs_n, 128)

    halo_wait(1)

    @pl.when(has_up)
    def _():
        place_x(0)

    @pl.when(has_down)
    def _():
        place_x(2)

    def pack(acc, s):
        parts = []
        for m in range(4):
            p = ((m // 2) * qs + 2 * s + m % 2) * SLOT
            parts.append(acc[p : p + PIECE])
        return jnp.concatenate(parts, axis=0).astype(jnp.bfloat16)

    def back(k, s):
        src = ms if k == 0 else igs
        dst = om_ref if k == 0 else oi_ref
        return remote(src.at[s], dst.at[j], o_send.at[k, s], o_recv.at[k, j], {"col": s})

    iacc[...] = jnp.zeros_like(iacc)
    for b in range(2):
        def body(t, carry):
            iacc[...] += jnp.dot(g_tap(b, t), k2[9 * b + t], preferred_element_type=jnp.float32)
            return carry

        lax.fori_loop(0, 9, body, 0)
    for s in range(n_col):
        igs[s] = pack(iacc, s)
    for s in cols:
        back(1, s).start()
    oi_ref[j] = igs[j]

    for b in range(2):
        macc[...] = jnp.zeros_like(macc)

        def body(t, carry):
            macc[...] += lax.dot_general(x_tap(b, t), k2[9 * b + t], (((1,), (1,)), ((), ())),
                                         preferred_element_type=jnp.float32)
            return carry

        lax.fori_loop(0, 9, body, 0)
        for s in range(n_col):
            ms[s, b] = pack(macc, s)
    for s in cols:
        back(0, s).start()
    om_ref[j] = ms[j]

    for b in (1, 0):
        us = pl.ds(18 * b, 18)
        total = sb[j, us]
        for i in range(1, n_col):
            s = lax.rem(j + n_col - i, n_col)
            remote(sb.at[s, us], rb_.at[s, us], r_send.at[1 + b, s], r_recv.at[1 + b, s], {"col": s}).wait_recv()
            total = total + rb_[s, us]
        tc[us] = total
    for zz in zs:
        cp = remote(tc.at[pl.ds(zz * per_z, per_z)], rc.at[z], r_send.at[3, zz], r_recv.at[3, z],
                    {"row": zz * 2 + c})
        cp.start()
        sends.append(cp)
    mine = tc[pl.ds(z * per_z, per_z)]
    for i in range(1, nz):
        zz = lax.rem(z + nz - i, nz)
        remote(tc.at[pl.ds(zz * per_z, per_z)], rc.at[zz], r_send.at[3, zz], r_recv.at[3, zz],
               {"row": zz * 2 + c}).wait_recv()
        mine = mine + rc[zz]
    fin[...] = mine * scale
    last = remote(fin, fx, r_send.at[4, 0], r_recv.at[4, 0], {"row": sib})
    last.start()
    ok_ref[:, c] = fin[...]
    last.wait()
    ok_ref[:, 1 - c] = fx[...]

    for k in range(2):
        for i in range(1, n_col):
            s = lax.rem(j + n_col - i, n_col)
            src = ms if k == 0 else igs
            dst = om_ref if k == 0 else oi_ref
            remote(src.at[s], dst.at[s], o_send.at[k, s], o_recv.at[k, s], {"col": s}).wait_recv()
        for s in cols:
            back(k, s).wait_send()
    for b in (1, 0):
        pair(b).wait_send()
        for s in cols:
            plane(b, s).wait_send()
    for cp in sends:
        cp.wait_send()
    halo_done(0)
    halo_done(1)


def phased(n_row, n_col, features, kernels, out_cotangent):
    nz = n_row // 2
    per_z = UNITS // nz
    chans = features.shape[2]
    outs_n = out_cotangent.shape[3]
    kk = 12 // n_col
    per_col = outs_n // n_col
    c = lax.axis_index("row") % 2
    bf, f32 = jnp.bfloat16, jnp.float32
    xs = features.reshape(2, 12, 2, n_col, kk, chans).transpose(3, 0, 2, 1, 4, 5)
    xs = xs.reshape(n_col, 4 * PIECE, chans)
    gs = out_cotangent.reshape(2, 2, 12, 2, n_col, kk, outs_n).transpose(4, 0, 1, 3, 2, 5, 6)
    gs = gs.reshape(n_col, 2, 4 * PIECE, outs_n)
    kt = kernels.T
    kt = jnp.where(c == 0, jnp.pad(kt, ((0, 0), (0, 64))), jnp.pad(kt, ((0, 0), (64, 0))))
    held = (per_z + 1) // 2
    ks = kt.reshape(per_col, held, 128).transpose(1, 0, 2)
    cells = features.shape[0] * n_row * features.shape[1] * n_col
    scale = 1.0 / float(cells) ** 0.5
    qs = 2 * n_col
    pix = 2 * qs * SLOT
    half = per_col // 2
    vm = pl.BlockSpec(memory_space=pltpu.VMEM)
    dma = pltpu.SemaphoreType.DMA
    om, oi, ok = pl.pallas_call(
        functools.partial(kernel, n_row, n_col, scale),
        out_shape=(
            jax.ShapeDtypeStruct((n_col, 2, 4 * PIECE, outs_n), bf),
            jax.ShapeDtypeStruct((n_col, 4 * PIECE, chans), bf),
            jax.ShapeDtypeStruct((per_z, 2, half, 128), f32),
        ),
        in_specs=[vm] * 3,
        out_specs=(vm,) * 3,
        scratch_shapes=[
            pltpu.VMEM((3, n_col, 2, 4 * PIECE, outs_n), bf),
            pltpu.VMEM((3, n_col, 4 * PIECE, chans), bf),
            pltpu.VMEM((2, 6, qs + 4, SLOT, outs_n), bf),
            pltpu.VMEM((6, qs + 4, SLOT, chans), bf),
            pltpu.VMEM((2, n_col, nz, held, per_col, 128), bf),
            pltpu.VMEM((18, outs_n, chans), bf),
            pltpu.VMEM((UNITS, n_col, 2, half, 128), f32),
            pltpu.VMEM((UNITS, n_col, half, 128), f32),
            pltpu.VMEM((n_col, UNITS, half, 128), f32),
            pltpu.VMEM((n_col, UNITS, half, 128), f32),
            pltpu.VMEM((UNITS, half, 128), f32),
            pltpu.VMEM((nz, per_z, half, 128), f32),
            pltpu.VMEM((per_z, half, 128), f32),
            pltpu.VMEM((per_z, half, 128), f32),
            pltpu.VMEM((pix, outs_n), f32),
            pltpu.VMEM((pix, chans), f32),
            pltpu.VMEM((n_col, 2, 4 * PIECE, outs_n), bf),
            pltpu.VMEM((n_col, 4 * PIECE, chans), bf),
            dma((2, n_col)), dma((2, n_col)),
            dma((2, 2, n_col)), dma((2, 2, n_col)),
            dma((3, max(n_col, nz))), dma((3, max(n_col, nz))),
            dma((2, n_col)), dma((2, n_col)),
            dma((5, max(n_col, nz))), dma((5, max(n_col, nz))),
        ],
        compiler_params=pltpu.CompilerParams(
            collective_id=0, has_side_effects=True, vmem_limit_bytes=48 * 1024 * 1024),
    )(gs, xs, ks)
    maps = om.reshape(n_col, 2, 2, 2, 12, kk, outs_n).transpose(1, 2, 4, 3, 0, 5, 6)
    maps = maps.reshape(2, 24, 24, outs_n)
    grad_in = oi.reshape(n_col, 2, 2, 12, kk, chans).transpose(1, 3, 2, 0, 4, 5)
    grad_in = grad_in.reshape(24, 24, chans)
    kg = ok.reshape(per_z, per_col, 128).transpose(1, 0, 2).reshape(per_col, per_z * 128)
    kg = jnp.where(c == 0, kg[:, : kernels.shape[0]], kg[:, per_z * 128 - kernels.shape[0] :])
    return maps, grad_in, kg.T


def with_halo(x, sides, width):
    for axis, dim in sides:
        size, length = (lax.axis_size(axis), x.shape[dim])
        up = [(i, (i + 1) % size) for i in range(size - 1)]
        down = [(j, i) for i, j in up]
        last = lax.slice_in_dim(x, length - width, length, axis=dim)
        initial = lax.slice_in_dim(x, 0, width, axis=dim)
        before = lax.ppermute(last, axis, up)
        after = lax.ppermute(initial, axis, down)
        x = jnp.concatenate([before, x, after], axis=dim)
    return x


def local(features, kernels, out_cotangent):
    rows_dev = features.shape[0]
    cols_dev = features.shape[1]
    chans = features.shape[2]
    outs_n = out_cotangent.shape[3]
    padding_margin = SECOND_SPACING
    x_ext = with_halo(features, (("row", 0), ("col", 1)), padding_margin)
    g_ext = with_halo(out_cotangent, (("row", 1), ("col", 2)), padding_margin)
    w_cols = lax.all_gather(kernels, "col", axis=1, tiled=True)
    w_full = lax.all_gather(w_cols, "row", axis=0, tiled=True)
    w_blocks = w_full.reshape(2, 9, chans, outs_n)
    pixels = rows_dev * cols_dev
    maps = []
    grads = []
    grad_in = jnp.zeros((pixels, chans), jnp.float32)
    for branch_index, dilation_rate in ((0, FIRST_SPACING), (1, SECOND_SPACING)):
        result = jnp.zeros((pixels, outs_n), jnp.float32)
        g_flat = out_cotangent[branch_index].reshape(pixels, outs_n)
        for kernel_tap in range(9):
            shift_down = (kernel_tap // 3 - 1) * dilation_rate
            shift_across = (kernel_tap % 3 - 1) * dilation_rate
            x_tap = x_ext[
                padding_margin + shift_down : padding_margin + shift_down + rows_dev,
                padding_margin + shift_across : padding_margin + shift_across + cols_dev,
            ].reshape(pixels, chans)
            g_tap = g_ext[
                branch_index,
                padding_margin - shift_down : padding_margin - shift_down + rows_dev,
                padding_margin - shift_across : padding_margin - shift_across + cols_dev,
            ].reshape(pixels, outs_n)
            weight = w_blocks[branch_index, kernel_tap]
            result = result + jnp.dot(x_tap, weight, preferred_element_type=jnp.float32)
            grad_in = grad_in + lax.dot_general(
                g_tap, weight, (((1,), (1,)), ((), ())), preferred_element_type=jnp.float32
            )
            grads.append(
                lax.dot_general(
                    x_tap, g_flat, (((0,), (0,)), ((), ())), preferred_element_type=jnp.float32
                )
            )
        maps.append(result.reshape(rows_dev, cols_dev, outs_n).astype(jnp.bfloat16))
    branch_maps = jnp.stack(maps, 0)
    input_grad = grad_in.reshape(rows_dev, cols_dev, chans).astype(jnp.bfloat16)
    local_grad = jnp.concatenate(grads, 0)
    total_cells = rows_dev * lax.axis_size("row") * cols_dev * lax.axis_size("col")
    scale = 1.0 / jnp.sqrt(jnp.float32(total_cells))
    partial_grad = lax.psum_scatter(local_grad, "row", scatter_dimension=0, tiled=True)
    kernel_grad = lax.psum_scatter(partial_grad, "col", scatter_dimension=1, tiled=True)
    return (branch_maps, input_grad, kernel_grad * scale)


def solution(mesh):
    n_row, n_col = mesh.shape["row"], mesh.shape["col"]
    fits = n_col == 4 and n_row == 8
    run = functools.partial(phased, n_row, n_col) if fits else local

    placed = (P("row", "col", None), P("row", "col"), P(None, "row", "col", None))
    return jax.shard_map(
        run,
        mesh=mesh,
        in_specs=placed,
        out_specs=(P(None, "row", "col", None), P("row", "col", None), P("row", "col")),
        check_vma=False,
    )
```

```python
import functools

import jax
import jax.numpy as jnp
from jax import lax
from jax.experimental import pallas as pl
from jax.experimental.pallas import tpu as pltpu
from jax.sharding import PartitionSpec as P

FIRST_SPACING = 12
SECOND_SPACING = 24
UNITS = 36
SLOT = 48
MESH = pl.DeviceIdType.MESH


def kernel(n_row, n_col, scale, gs_ref, xs_ref, ks_ref, om_ref, oi_ref, ok_ref,
           ga, xa, gp, xp, kb, k2, ru, ra, sb, rb1, rb2, tc, rc, fin, fx, macc, iacc, ms, igs,
           a_send, a_recv, h_send, h_recv, k_send, k_recv, o_send, o_recv,
           p_send, p_recv, s_send, s_recv, q_send, q_recv, z_send, z_recv, l_send, l_recv):
    nz = n_row // 2
    per_z = UNITS // nz
    r = lax.axis_index("row")
    j = lax.axis_index("col")
    z = r // 2
    c = r % 2
    sib = r + 1 - 2 * c
    cols = [lax.rem(j + i, n_col) for i in range(1, n_col)]
    zs = [lax.rem(z + i, nz) for i in range(1, nz)]
    across = j + 1 - 2 * (j % 2)
    along = j + 2 - 4 * (j // 2)
    first = jnp.where(c == 0, across, along)
    second = jnp.where(c == 0, along, across)
    corner = first + second - j
    far = r - 1 + 2 * c
    has_up = r > 0
    has_down = r < n_row - 1
    has_far = jnp.where(c == 0, has_up, has_down)

    barrier = pltpu.get_barrier_semaphore()
    for s in cols:
        pl.semaphore_signal(barrier, inc=1, device_id={"col": s}, device_id_type=MESH)
    for zz in zs:
        pl.semaphore_signal(barrier, inc=1, device_id={"row": zz * 2 + c}, device_id_type=MESH)
    pl.semaphore_signal(barrier, inc=1, device_id={"row": sib}, device_id_type=MESH)

    @pl.when(has_far)
    def _():
        pl.semaphore_signal(barrier, inc=1, device_id={"row": far}, device_id_type=MESH)

    pl.semaphore_wait(barrier, n_col - 1 + nz - 1 + 1 + jnp.where(has_far, 1, 0))

    def remote(src, dst, ssem, rsem, dev):
        return pltpu.make_async_remote_copy(
            src_ref=src, dst_ref=dst, send_sem=ssem, recv_sem=rsem,
            device_id=dev, device_id_type=MESH)

    def deal(a, s):
        if a == 0:
            src, dst = gs_ref.at[:, :, s], ga.at[1, j]
        else:
            src, dst = xs_ref.at[:, s], xa.at[1, j]
        return remote(src, dst, a_send.at[a, s], a_recv.at[a, j], {"col": s})

    def dealt(a, s):
        if a == 0:
            src, dst = gs_ref.at[:, :, s], ga.at[1, s]
        else:
            src, dst = xs_ref.at[:, s], xa.at[1, s]
        return remote(src, dst, a_send.at[a, s], a_recv.at[a, s], {"col": s})

    sends = []

    def go(cp):
        cp.start()
        sends.append(cp)

    for s in cols:
        go(deal(0, s))
    for zz in zs:
        go(remote(ks_ref, kb.at[c, j, z], k_send.at[0, zz], k_recv.at[0, z], {"row": zz * 2 + c}))
    for s in cols:
        go(deal(1, s))
    kb[c, j, z] = ks_ref[...]
    ga[1, j] = gs_ref[:, :, j]
    xa[1, j] = xs_ref[:, j]

    def halo(a, s, up):
        buf = ga if a == 0 else xa
        to = r - 1 if up else r + 1
        d = 0 if up else 1
        return remote(buf.at[1, s], buf.at[2 if up else 0, s],
                      h_send.at[a, d, s], h_recv.at[a, d, s], {"row": to})

    def spread(a, s):
        @pl.when(has_up)
        def _():
            halo(a, s, True).start()

        @pl.when(has_down)
        def _():
            halo(a, s, False).start()

    def gather(a):
        for i in range(1, n_col):
            s = lax.rem(j + n_col - i, n_col)
            dealt(a, s).wait_recv()
            spread(a, s)

    def halo_wait(a):
        for s in range(n_col):
            @pl.when(has_down)
            def _():
                halo(a, s, True).wait_recv()

            @pl.when(has_up)
            def _():
                halo(a, s, False).wait_recv()

    def halo_done(a):
        for s in range(n_col):
            @pl.when(has_up)
            def _():
                halo(a, s, True).wait_send()

            @pl.when(has_down)
            def _():
                halo(a, s, False).wait_send()

    spread(0, j)
    gp[...] = jnp.zeros_like(gp)
    xp[...] = jnp.zeros_like(xp)
    gather(0)
    for i in range(1, nz):
        zz = lax.rem(z + nz - i, nz)
        remote(ks_ref, kb.at[c, j, zz], k_send.at[0, zz], k_recv.at[0, zz], {"row": zz * 2 + c}).wait_recv()

    def share(n, s, to):
        return remote(kb.at[c, s], kb.at[c, s], k_send.at[1, n], k_recv.at[1, n], {"col": to})

    go(share(0, j, first))
    go(share(1, j, second))
    spread(1, j)
    gather(1)

    def place(n):
        for s in range(n_col):
            for b in range(2):
                block = ga[n, s, b].astype(jnp.float32)
                for h in range(2):
                    part = block[:, :, 12 * h : 12 * (h + 1)].astype(jnp.bfloat16)
                    gp[b, 2 * n : 2 * n + 2, 2 + 2 * s + h, :, 0:12, :] = part

    def place_x(n):
        for s in range(n_col):
            block = xa[n, s].astype(jnp.float32)
            for h in range(2):
                part = block[:, :, 12 * h : 12 * (h + 1)].astype(jnp.bfloat16)
                xp[2 * n : 2 * n + 2, 2 + 2 * s + h, :, 0:12, :] = part

    place(1)
    place_x(1)
    share(0, first, first).wait_recv()
    go(share(2, first, second))
    halo_wait(0)

    @pl.when(has_up)
    def _():
        place(0)

    @pl.when(has_down)
    def _():
        place(2)

    qs = 2 * n_col
    outs_n = gp.shape[-1]
    chans = xp.shape[-1]
    pix = 2 * qs * SLOT
    half = outs_n // n_col // 2

    def g_tap(b, t):
        d = 1 + b
        sy = (t // 3 - 1) * d
        sx = (t % 3 - 1) * d
        return gp[b, pl.ds(2 - sy, 2), pl.ds(2 - sx, qs)].reshape(pix, outs_n)

    def x_tap(b, t):
        d = 1 + b
        sy = (t // 3 - 1) * d
        sx = (t % 3 - 1) * d
        return xp[pl.ds(2 + sy, 2), pl.ds(2 + sx, qs)].reshape(pix, chans)

    def pair(b):
        us = pl.ds(18 * b, 18)
        return remote(ru.at[us, :, 1 - c], ra.at[us], p_send.at[b], p_recv.at[b], {"row": sib})

    def step(b, k):
        us = pl.ds(18 * b, 18)
        return remote(sb.at[first if k == 0 else corner, us], rb1.at[k, us],
                      s_send.at[b, k], s_recv.at[b, k], {"col": first})

    def close(b):
        us = pl.ds(18 * b, 18)
        return remote(sb.at[second, us], rb2.at[us], q_send.at[b], q_recv.at[b], {"col": second})

    def spine(zz, at):
        return remote(tc.at[pl.ds(zz * per_z, per_z)], rc.at[at], z_send.at[zz], z_recv.at[at],
                      {"row": zz * 2 + c})

    for b in (1, 0):
        def body(t, carry):
            x_here = xp[pl.ds(2, 2), pl.ds(2, qs)].reshape(pix, chans)
            res = lax.dot_general(g_tap(b, t), x_here, (((0,), (0,)), ((), ())),
                                  preferred_element_type=jnp.float32)
            for h in range(2):
                ru[2 * (9 * b + t) + h] = res[:, 128 * h : 128 * (h + 1)].reshape(n_col, 2, half, 128)
            return carry

        lax.fori_loop(0, 9, body, 0)
        pair(b).start()

    for b in (1, 0):
        us = pl.ds(18 * b, 18)
        pair(b).wait_recv()
        for s in range(n_col):
            sb[s, us] = ru[us, s, c] + ra[us, s]
        for k in (1, 0):
            step(b, k).start()

    share(1, second, second).wait_recv()
    share(2, corner, second).wait_recv()
    swap = remote(kb.at[c], kb.at[c], k_send.at[2, 0], k_recv.at[2, 0], {"row": sib})
    go(swap)

    def reduce_plane(b):
        us = pl.ds(18 * b, 18)
        step(b, 1).wait_recv()
        sb[second, us] = sb[second, us] + rb1[1, us]
        close(b).start()
        step(b, 0).wait_recv()
        sb[j, us] = sb[j, us] + rb1[0, us]

    def reduce_spine(b):
        us = pl.ds(18 * b, 18)
        close(b).wait_recv()
        tc[us] = sb[j, us] + rb2[us]
        for zz in zs:
            @pl.when(zz // (nz // 2) == b)
            def _():
                spine(zz, z).start()

    reduce_plane(1)
    remote(kb.at[1 - c], kb.at[1 - c], k_send.at[2, 0], k_recv.at[2, 0], {"row": sib}).wait_recv()
    for u in range(UNITS):
        zz, v = divmod(u, per_z)
        mid = per_z // 2
        if v < mid:
            val = kb[0, :, zz, v]
        elif v > mid:
            val = kb[1, :, zz, v - mid]
        else:
            val = kb[0, :, zz, mid] + kb[1, :, zz, 0]
        k2[u // 2, :, 128 * (u % 2) : 128 * (u % 2 + 1)] = val.reshape(outs_n, 128)

    def pack(acc, s):
        halves = [acc[:, 2 * s + h, :, 0:12, :] for h in range(2)]
        return jnp.concatenate(halves, axis=2).astype(jnp.bfloat16)

    def back(k, s, at):
        if k == 2:
            src, dst = igs.at[s], oi_ref.at[:, at]
        else:
            src, dst = ms.at[s, k], om_ref.at[k, :, at]
        return remote(src, dst, o_send.at[k, s], o_recv.at[k, at], {"col": s})

    def input_part(b):
        def body(t, carry):
            res = jnp.dot(g_tap(b, t), k2[9 * b + t], preferred_element_type=jnp.float32)
            iacc[...] += res.reshape(iacc.shape)
            return carry

        lax.fori_loop(0, 9, body, 0)

    def map_part(b):
        macc[...] = jnp.zeros_like(macc)

        def body(t, carry):
            res = lax.dot_general(x_tap(b, t), k2[9 * b + t], (((1,), (1,)), ((), ())),
                                  preferred_element_type=jnp.float32)
            macc[...] += res.reshape(macc.shape)
            return carry

        lax.fori_loop(0, 9, body, 0)
        for s in range(n_col):
            ms[s, b] = pack(macc, s)
        for s in cols:
            back(b, s, j).start()
        om_ref[b, :, j] = ms[j, b]

    iacc[...] = jnp.zeros_like(iacc)
    input_part(0)
    reduce_plane(0)
    input_part(1)
    for s in range(n_col):
        igs[s] = pack(iacc, s)
    for s in cols:
        back(2, s, j).start()
    oi_ref[:, j] = igs[j]
    reduce_spine(1)

    halo_wait(1)

    @pl.when(has_up)
    def _():
        place_x(0)

    @pl.when(has_down)
    def _():
        place_x(2)

    map_part(0)
    reduce_spine(0)
    map_part(1)

    mine = tc[pl.ds(z * per_z, per_z)]
    for i in range(1, nz):
        zz = lax.rem(z + nz - i, nz)
        spine(zz, zz).wait_recv()
        mine = mine + rc[zz]
    fin[...] = mine * scale
    last = remote(fin, fx, l_send.at[0], l_recv.at[0], {"row": sib})
    last.start()
    ok_ref[:, c] = fin[...]
    last.wait()
    ok_ref[:, 1 - c] = fx[...]

    for k in range(3):
        for i in range(1, n_col):
            s = lax.rem(j + n_col - i, n_col)
            back(k, s, s).wait_recv()
        for s in cols:
            back(k, s, j).wait_send()
    for b in (1, 0):
        pair(b).wait_send()
        for k in (1, 0):
            step(b, k).wait_send()
        close(b).wait_send()
    for zz in zs:
        spine(zz, z).wait_send()
    for cp in sends:
        cp.wait_send()
    halo_done(0)
    halo_done(1)


def phased(n_row, n_col, features, kernels, out_cotangent):
    nz = n_row // 2
    per_z = UNITS // nz
    rows_dev, cols_dev, chans = features.shape
    outs_n = out_cotangent.shape[3]
    kk = 12 // n_col
    per_col = outs_n // n_col
    c = lax.axis_index("row") % 2
    bf, f32 = jnp.bfloat16, jnp.float32
    xs = features.reshape(2, n_col, kk, cols_dev, chans)
    gs = out_cotangent.reshape(2, 2, n_col, kk, cols_dev, outs_n)
    kt = kernels.T
    kt = jnp.where(c == 0, jnp.pad(kt, ((0, 0), (0, 64))), jnp.pad(kt, ((0, 0), (64, 0))))
    held = (per_z + 1) // 2
    ks = kt.reshape(per_col, held, 128).transpose(1, 0, 2)
    cells = rows_dev * n_row * cols_dev * n_col
    scale = 1.0 / float(cells) ** 0.5
    qs = 2 * n_col
    half = per_col // 2
    vm = pl.BlockSpec(memory_space=pltpu.VMEM)
    dma = pltpu.SemaphoreType.DMA
    om, oi, ok = pl.pallas_call(
        functools.partial(kernel, n_row, n_col, scale),
        out_shape=(
            jax.ShapeDtypeStruct(gs.shape, bf),
            jax.ShapeDtypeStruct(xs.shape, bf),
            jax.ShapeDtypeStruct((per_z, 2, half, 128), f32),
        ),
        in_specs=[vm] * 3,
        out_specs=(vm,) * 3,
        scratch_shapes=[
            pltpu.VMEM((3, n_col, 2, 2, kk, cols_dev, outs_n), bf),
            pltpu.VMEM((3, n_col, 2, kk, cols_dev, chans), bf),
            pltpu.VMEM((2, 6, qs + 4, kk, 16, outs_n), bf),
            pltpu.VMEM((6, qs + 4, kk, 16, chans), bf),
            pltpu.VMEM((2, n_col, nz, held, per_col, 128), bf),
            pltpu.VMEM((18, outs_n, chans), bf),
            pltpu.VMEM((UNITS, n_col, 2, half, 128), f32),
            pltpu.VMEM((UNITS, n_col, half, 128), f32),
            pltpu.VMEM((n_col, UNITS, half, 128), f32),
            pltpu.VMEM((2, UNITS, half, 128), f32),
            pltpu.VMEM((UNITS, half, 128), f32),
            pltpu.VMEM((UNITS, half, 128), f32),
            pltpu.VMEM((nz, per_z, half, 128), f32),
            pltpu.VMEM((per_z, half, 128), f32),
            pltpu.VMEM((per_z, half, 128), f32),
            pltpu.VMEM((2, qs, kk, 16, outs_n), f32),
            pltpu.VMEM((2, qs, kk, 16, chans), f32),
            pltpu.VMEM((n_col, 2, 2, kk, cols_dev, outs_n), bf),
            pltpu.VMEM((n_col, 2, kk, cols_dev, chans), bf),
            dma((2, n_col)), dma((2, n_col)),
            dma((2, 2, n_col)), dma((2, 2, n_col)),
            dma((3, 4)), dma((3, 4)),
            dma((3, n_col)), dma((3, n_col)),
            dma((2,)), dma((2,)),
            dma((2, 2)), dma((2, 2)),
            dma((2,)), dma((2,)),
            dma((nz,)), dma((nz,)),
            dma((1,)), dma((1,)),
        ],
        compiler_params=pltpu.CompilerParams(
            collective_id=0, has_side_effects=True, vmem_limit_bytes=48 * 1024 * 1024),
    )(gs, xs, ks)
    kg = ok.reshape(per_z, per_col, 128).transpose(1, 0, 2).reshape(per_col, per_z * 128)
    kg = jnp.where(c == 0, kg[:, : kernels.shape[0]], kg[:, per_z * 128 - kernels.shape[0] :])
    return om.reshape(out_cotangent.shape), oi.reshape(features.shape), kg.T


def with_halo(x, sides, width):
    for axis, dim in sides:
        size, length = (lax.axis_size(axis), x.shape[dim])
        up = [(i, (i + 1) % size) for i in range(size - 1)]
        down = [(j, i) for i, j in up]
        last = lax.slice_in_dim(x, length - width, length, axis=dim)
        initial = lax.slice_in_dim(x, 0, width, axis=dim)
        before = lax.ppermute(last, axis, up)
        after = lax.ppermute(initial, axis, down)
        x = jnp.concatenate([before, x, after], axis=dim)
    return x


def local(features, kernels, out_cotangent):
    rows_dev = features.shape[0]
    cols_dev = features.shape[1]
    chans = features.shape[2]
    outs_n = out_cotangent.shape[3]
    padding_margin = SECOND_SPACING
    x_ext = with_halo(features, (("row", 0), ("col", 1)), padding_margin)
    g_ext = with_halo(out_cotangent, (("row", 1), ("col", 2)), padding_margin)
    w_cols = lax.all_gather(kernels, "col", axis=1, tiled=True)
    w_full = lax.all_gather(w_cols, "row", axis=0, tiled=True)
    w_blocks = w_full.reshape(2, 9, chans, outs_n)
    pixels = rows_dev * cols_dev
    maps = []
    grads = []
    grad_in = jnp.zeros((pixels, chans), jnp.float32)
    for branch_index, dilation_rate in ((0, FIRST_SPACING), (1, SECOND_SPACING)):
        result = jnp.zeros((pixels, outs_n), jnp.float32)
        g_flat = out_cotangent[branch_index].reshape(pixels, outs_n)
        for kernel_tap in range(9):
            shift_down = (kernel_tap // 3 - 1) * dilation_rate
            shift_across = (kernel_tap % 3 - 1) * dilation_rate
            x_tap = x_ext[
                padding_margin + shift_down : padding_margin + shift_down + rows_dev,
                padding_margin + shift_across : padding_margin + shift_across + cols_dev,
            ].reshape(pixels, chans)
            g_tap = g_ext[
                branch_index,
                padding_margin - shift_down : padding_margin - shift_down + rows_dev,
                padding_margin - shift_across : padding_margin - shift_across + cols_dev,
            ].reshape(pixels, outs_n)
            weight = w_blocks[branch_index, kernel_tap]
            result = result + jnp.dot(x_tap, weight, preferred_element_type=jnp.float32)
            grad_in = grad_in + lax.dot_general(
                g_tap, weight, (((1,), (1,)), ((), ())), preferred_element_type=jnp.float32
            )
            grads.append(
                lax.dot_general(
                    x_tap, g_flat, (((0,), (0,)), ((), ())), preferred_element_type=jnp.float32
                )
            )
        maps.append(result.reshape(rows_dev, cols_dev, outs_n).astype(jnp.bfloat16))
    branch_maps = jnp.stack(maps, 0)
    input_grad = grad_in.reshape(rows_dev, cols_dev, chans).astype(jnp.bfloat16)
    local_grad = jnp.concatenate(grads, 0)
    total_cells = rows_dev * lax.axis_size("row") * cols_dev * lax.axis_size("col")
    scale = 1.0 / jnp.sqrt(jnp.float32(total_cells))
    partial_grad = lax.psum_scatter(local_grad, "row", scatter_dimension=0, tiled=True)
    kernel_grad = lax.psum_scatter(partial_grad, "col", scatter_dimension=1, tiled=True)
    return (branch_maps, input_grad, kernel_grad * scale)


def solution(mesh):
    n_row, n_col = mesh.shape["row"], mesh.shape["col"]
    fits = n_col == 4 and n_row == 8
    run = functools.partial(phased, n_row, n_col) if fits else local

    placed = (P("row", "col", None), P("row", "col"), P(None, "row", "col", None))
    return jax.shard_map(
        run,
        mesh=mesh,
        in_specs=placed,
        out_specs=(P(None, "row", "col", None), P("row", "col", None), P("row", "col")),
        check_vma=False,
    )
```

```python
import functools

import jax
import jax.numpy as jnp
from jax import lax
from jax.experimental import pallas as pl
from jax.experimental.pallas import tpu as pltpu
from jax.sharding import PartitionSpec as P

FIRST_SPACING = 12
SECOND_SPACING = 24
UNITS = 36
SLOT = 48
MESH = pl.DeviceIdType.MESH


def kernel(n_row, n_col, scale, gs_ref, xs_ref, ks_ref, om_ref, oi_ref, ok_ref,
           ga, xa, gp, xp, kb, k2, ru, ra, sb, rb1, rb2, tc, rc, fin, fx, macc, iacc, ms, igs,
           a_send, a_recv, h_send, h_recv, k_send, k_recv, o_send, o_recv,
           p_send, p_recv, s_send, s_recv, q_send, q_recv, z_send, z_recv, l_send, l_recv, own_sem):
    nz = n_row // 2
    per_z = UNITS // nz
    r = lax.axis_index("row")
    j = lax.axis_index("col")
    z = r // 2
    c = r % 2
    sib = r + 1 - 2 * c
    cols = [lax.rem(j + i, n_col) for i in range(1, n_col)]
    zs = [lax.rem(z + i, nz) for i in range(1, nz)]
    across = j + 1 - 2 * (j % 2)
    along = j + 2 - 4 * (j // 2)
    first = jnp.where(c == 0, across, along)
    second = jnp.where(c == 0, along, across)
    corner = first + second - j
    far = r - 1 + 2 * c
    has_up = r > 0
    has_down = r < n_row - 1
    has_far = jnp.where(c == 0, has_up, has_down)

    barrier = pltpu.get_barrier_semaphore()
    for s in cols:
        pl.semaphore_signal(barrier, inc=1, device_id={"col": s}, device_id_type=MESH)
    for zz in zs:
        pl.semaphore_signal(barrier, inc=1, device_id={"row": zz * 2 + c}, device_id_type=MESH)
    pl.semaphore_signal(barrier, inc=1, device_id={"row": sib}, device_id_type=MESH)

    @pl.when(has_far)
    def _():
        pl.semaphore_signal(barrier, inc=1, device_id={"row": far}, device_id_type=MESH)

    pl.semaphore_wait(barrier, n_col - 1 + nz - 1 + 1 + jnp.where(has_far, 1, 0))

    def remote(src, dst, ssem, rsem, dev):
        return pltpu.make_async_remote_copy(
            src_ref=src, dst_ref=dst, send_sem=ssem, recv_sem=rsem,
            device_id=dev, device_id_type=MESH)

    def deal(a, s):
        if a == 0:
            src, dst = gs_ref.at[:, :, s], ga.at[1, j]
        else:
            src, dst = xs_ref.at[:, s], xa.at[1, j]
        return remote(src, dst, a_send.at[a, s], a_recv.at[a, j], {"col": s})

    def dealt(a, s):
        if a == 0:
            src, dst = gs_ref.at[:, :, s], ga.at[1, s]
        else:
            src, dst = xs_ref.at[:, s], xa.at[1, s]
        return remote(src, dst, a_send.at[a, s], a_recv.at[a, s], {"col": s})

    sends = []

    def go(cp):
        cp.start()
        sends.append(cp)

    for s in cols:
        go(deal(0, s))
    for zz in zs:
        go(remote(ks_ref, kb.at[c, j, z], k_send.at[0, zz], k_recv.at[0, z], {"row": zz * 2 + c}))
    for s in cols:
        go(deal(1, s))
    kb[c, j, z] = ks_ref[...]
    own_g = pltpu.make_async_copy(gs_ref.at[:, :, j], ga.at[1, j], own_sem.at[0])
    own_x = pltpu.make_async_copy(xs_ref.at[:, j], xa.at[1, j], own_sem.at[1])
    own_g.start()
    own_x.start()

    def halo(a, s, up):
        buf = ga if a == 0 else xa
        to = r - 1 if up else r + 1
        d = 0 if up else 1
        return remote(buf.at[1, s], buf.at[2 if up else 0, s],
                      h_send.at[a, d, s], h_recv.at[a, d, s], {"row": to})

    def spread(a, s):
        @pl.when(has_up)
        def _():
            halo(a, s, True).start()

        @pl.when(has_down)
        def _():
            halo(a, s, False).start()

    def gather(a):
        for i in range(1, n_col):
            s = lax.rem(j + n_col - i, n_col)
            dealt(a, s).wait_recv()
            spread(a, s)

    def halo_wait(a):
        for s in range(n_col):
            @pl.when(has_down)
            def _():
                halo(a, s, True).wait_recv()

            @pl.when(has_up)
            def _():
                halo(a, s, False).wait_recv()

    def halo_done(a):
        for s in range(n_col):
            @pl.when(has_up)
            def _():
                halo(a, s, True).wait_send()

            @pl.when(has_down)
            def _():
                halo(a, s, False).wait_send()

    gp[...] = jnp.zeros_like(gp)
    xp[...] = jnp.zeros_like(xp)
    own_g.wait()
    spread(0, j)
    gather(0)
    for i in range(1, nz):
        zz = lax.rem(z + nz - i, nz)
        remote(ks_ref, kb.at[c, j, zz], k_send.at[0, zz], k_recv.at[0, zz], {"row": zz * 2 + c}).wait_recv()

    def share(n, s, to):
        return remote(kb.at[c, s], kb.at[c, s], k_send.at[1, n], k_recv.at[1, n], {"col": to})

    go(share(0, j, first))
    go(share(1, j, second))
    own_x.wait()
    spread(1, j)
    gather(1)

    def place(n):
        for s in range(n_col):
            for b in range(2):
                block = ga[n, s, b].astype(jnp.float32)
                for h in range(2):
                    part = block[:, :, 12 * h : 12 * (h + 1)].astype(jnp.bfloat16)
                    gp[b, 2 * n : 2 * n + 2, 2 + 2 * s + h, :, 0:12, :] = part

    def place_x(n):
        for s in range(n_col):
            block = xa[n, s].astype(jnp.float32)
            for h in range(2):
                part = block[:, :, 12 * h : 12 * (h + 1)].astype(jnp.bfloat16)
                xp[2 * n : 2 * n + 2, 2 + 2 * s + h, :, 0:12, :] = part

    qs = 2 * n_col
    outs_n = gp.shape[-1]
    chans = xp.shape[-1]
    pix = 2 * qs * SLOT
    half = outs_n // n_col // 2

    def g_tap(b, t):
        d = 1 + b
        sy = (t // 3 - 1) * d
        sx = (t % 3 - 1) * d
        return gp[b, pl.ds(2 - sy, 2), pl.ds(2 - sx, qs)].reshape(pix, outs_n)

    def x_tap(b, t):
        d = 1 + b
        sy = (t // 3 - 1) * d
        sx = (t % 3 - 1) * d
        return xp[pl.ds(2 + sy, 2), pl.ds(2 + sx, qs)].reshape(pix, chans)

    def span(g):
        return pl.ds(6 * g, 6)

    def pair(g):
        us = span(g)
        return remote(ru.at[us, :, 1 - c], ra.at[us], p_send.at[g], p_recv.at[g], {"row": sib})

    def step(g, k):
        us = span(g)
        return remote(sb.at[first if k == 0 else corner, us], rb1.at[k, us],
                      s_send.at[g, k], s_recv.at[g, k], {"col": first})

    def close(g):
        us = span(g)
        return remote(sb.at[second, us], rb2.at[us], q_send.at[g], q_recv.at[g], {"col": second})

    def spine(zz, k, at):
        return remote(tc.at[pl.ds(zz * per_z + 3 * k, 3)], rc.at[at, pl.ds(3 * k, 3)],
                      z_send.at[k, zz], z_recv.at[k, at], {"row": zz * 2 + c})

    def taps_grad(g):
        b = g // 3

        def body(i, carry):
            t = 3 * (g % 3) + i
            x_here = xp[pl.ds(2, 2), pl.ds(2, qs)].reshape(pix, chans)
            res = lax.dot_general(g_tap(b, t), x_here, (((0,), (0,)), ((), ())),
                                  preferred_element_type=jnp.float32)
            for h in range(2):
                ru[2 * (9 * b + t) + h] = res[:, 128 * h : 128 * (h + 1)].reshape(n_col, 2, half, 128)
            return carry

        lax.fori_loop(0, 3, body, 0)
        pair(g).start()

    def reduce_pair(g):
        us = span(g)
        pair(g).wait_recv()
        for s in range(n_col):
            sb[s, us] = ru[us, s, c] + ra[us, s]
        for k in (1, 0):
            step(g, k).start()

    def reduce_plane(g):
        us = span(g)
        step(g, 1).wait_recv()
        sb[second, us] = sb[second, us] + rb1[1, us]
        close(g).start()
        step(g, 0).wait_recv()
        sb[j, us] = sb[j, us] + rb1[0, us]

    def reduce_spine(g):
        us = span(g)
        close(g).wait_recv()
        tc[us] = sb[j, us] + rb2[us]
        for q in (2 * g, 2 * g + 1):
            @pl.when(z != 3 * q // per_z)
            def _():
                spine(3 * q // per_z, q % (per_z // 3), z).start()

    place(1)
    place_x(1)
    taps_grad(1)
    share(0, first, first).wait_recv()
    taps_grad(4)
    reduce_pair(1)
    halo_wait(0)

    @pl.when(has_up)
    def _():
        place(0)

    @pl.when(has_down)
    def _():
        place(2)

    reduce_pair(4)
    taps_grad(3)
    go(share(2, first, second))
    reduce_plane(1)
    taps_grad(5)
    reduce_pair(3)
    reduce_plane(4)
    taps_grad(0)
    reduce_pair(5)
    reduce_spine(1)
    taps_grad(2)
    reduce_pair(0)
    reduce_plane(3)
    reduce_spine(4)
    reduce_pair(2)
    reduce_plane(5)

    share(1, second, second).wait_recv()
    share(2, corner, second).wait_recv()
    swap = remote(kb.at[c], kb.at[c], k_send.at[2, 0], k_recv.at[2, 0], {"row": sib})
    go(swap)
    reduce_spine(3)
    reduce_plane(0)
    remote(kb.at[1 - c], kb.at[1 - c], k_send.at[2, 0], k_recv.at[2, 0], {"row": sib}).wait_recv()
    for u in range(UNITS):
        zz, v = divmod(u, per_z)
        mid = per_z // 2
        if v < mid:
            val = kb[0, :, zz, v]
        elif v > mid:
            val = kb[1, :, zz, v - mid]
        else:
            val = kb[0, :, zz, mid] + kb[1, :, zz, 0]
        k2[u // 2, :, 128 * (u % 2) : 128 * (u % 2 + 1)] = val.reshape(outs_n, 128)

    def pack(acc, s):
        halves = [acc[:, 2 * s + h, :, 0:12, :] for h in range(2)]
        return jnp.concatenate(halves, axis=2).astype(jnp.bfloat16)

    def back(k, s, at):
        if k == 2:
            src, dst = igs.at[s], oi_ref.at[:, at]
        else:
            src, dst = ms.at[s, k], om_ref.at[k, :, at]
        return remote(src, dst, o_send.at[k, s], o_recv.at[k, at], {"col": s})

    def input_part(b):
        def body(t, carry):
            res = jnp.dot(g_tap(b, t), k2[9 * b + t], preferred_element_type=jnp.float32)
            iacc[...] += res.reshape(iacc.shape)
            return carry

        lax.fori_loop(0, 9, body, 0)

    def map_part(b):
        macc[...] = jnp.zeros_like(macc)

        def body(t, carry):
            res = lax.dot_general(x_tap(b, t), k2[9 * b + t], (((1,), (1,)), ((), ())),
                                  preferred_element_type=jnp.float32)
            macc[...] += res.reshape(macc.shape)
            return carry

        lax.fori_loop(0, 9, body, 0)
        for s in range(n_col):
            ms[s, b] = pack(macc, s)
        for s in cols:
            back(b, s, j).start()
        om_ref[b, :, j] = ms[j, b]

    iacc[...] = jnp.zeros_like(iacc)
    input_part(0)
    reduce_plane(2)
    reduce_spine(5)
    reduce_spine(0)
    input_part(1)
    for s in range(n_col):
        igs[s] = pack(iacc, s)
    for s in cols:
        back(2, s, j).start()
    oi_ref[:, j] = igs[j]
    reduce_spine(2)

    halo_wait(1)

    @pl.when(has_up)
    def _():
        place_x(0)

    @pl.when(has_down)
    def _():
        place_x(2)

    map_part(0)
    mine = tc[pl.ds(z * per_z, per_z)]
    for i in range(1, nz):
        zz = lax.rem(z + nz - i, nz)
        for k in range(per_z // 3):
            spine(zz, k, zz).wait_recv()
        mine = mine + rc[zz]
    fin[...] = mine * scale
    last = remote(fin, fx, l_send.at[0], l_recv.at[0], {"row": sib})
    last.start()
    ok_ref[:, c] = fin[...]
    map_part(1)
    last.wait()
    ok_ref[:, 1 - c] = fx[...]

    for k in range(3):
        for i in range(1, n_col):
            s = lax.rem(j + n_col - i, n_col)
            back(k, s, s).wait_recv()
        for s in cols:
            back(k, s, j).wait_send()
    for g in range(6):
        pair(g).wait_send()
        for k in (1, 0):
            step(g, k).wait_send()
        close(g).wait_send()
    for zz in zs:
        for k in range(per_z // 3):
            spine(zz, k, z).wait_send()
    for cp in sends:
        cp.wait_send()
    halo_done(0)
    halo_done(1)


def phased(n_row, n_col, features, kernels, out_cotangent):
    nz = n_row // 2
    per_z = UNITS // nz
    rows_dev, cols_dev, chans = features.shape
    outs_n = out_cotangent.shape[3]
    kk = 12 // n_col
    per_col = outs_n // n_col
    c = lax.axis_index("row") % 2
    bf, f32 = jnp.bfloat16, jnp.float32
    xs = features.reshape(2, n_col, kk, cols_dev, chans)
    gs = out_cotangent.reshape(2, 2, n_col, kk, cols_dev, outs_n)
    kt = kernels.T
    kt = jnp.where(c == 0, jnp.pad(kt, ((0, 0), (0, 64))), jnp.pad(kt, ((0, 0), (64, 0))))
    held = (per_z + 1) // 2
    ks = kt.reshape(per_col, held, 128).transpose(1, 0, 2)
    cells = rows_dev * n_row * cols_dev * n_col
    scale = 1.0 / float(cells) ** 0.5
    qs = 2 * n_col
    half = per_col // 2
    vm = pl.BlockSpec(memory_space=pltpu.VMEM)
    dma = pltpu.SemaphoreType.DMA
    om, oi, ok = pl.pallas_call(
        functools.partial(kernel, n_row, n_col, scale),
        out_shape=(
            jax.ShapeDtypeStruct(gs.shape, bf),
            jax.ShapeDtypeStruct(xs.shape, bf),
            jax.ShapeDtypeStruct((per_z, 2, half, 128), f32),
        ),
        in_specs=[pl.BlockSpec(memory_space=pltpu.HBM)] * 2 + [vm],
        out_specs=(vm,) * 3,
        scratch_shapes=[
            pltpu.VMEM((3, n_col, 2, 2, kk, cols_dev, outs_n), bf),
            pltpu.VMEM((3, n_col, 2, kk, cols_dev, chans), bf),
            pltpu.VMEM((2, 6, qs + 4, kk, 16, outs_n), bf),
            pltpu.VMEM((6, qs + 4, kk, 16, chans), bf),
            pltpu.VMEM((2, n_col, nz, held, per_col, 128), bf),
            pltpu.VMEM((18, outs_n, chans), bf),
            pltpu.VMEM((UNITS, n_col, 2, half, 128), f32),
            pltpu.VMEM((UNITS, n_col, half, 128), f32),
            pltpu.VMEM((n_col, UNITS, half, 128), f32),
            pltpu.VMEM((2, UNITS, half, 128), f32),
            pltpu.VMEM((UNITS, half, 128), f32),
            pltpu.VMEM((UNITS, half, 128), f32),
            pltpu.VMEM((nz, per_z, half, 128), f32),
            pltpu.VMEM((per_z, half, 128), f32),
            pltpu.VMEM((per_z, half, 128), f32),
            pltpu.VMEM((2, qs, kk, 16, outs_n), f32),
            pltpu.VMEM((2, qs, kk, 16, chans), f32),
            pltpu.VMEM((n_col, 2, 2, kk, cols_dev, outs_n), bf),
            pltpu.VMEM((n_col, 2, kk, cols_dev, chans), bf),
            dma((2, n_col)), dma((2, n_col)),
            dma((2, 2, n_col)), dma((2, 2, n_col)),
            dma((3, 4)), dma((3, 4)),
            dma((3, n_col)), dma((3, n_col)),
            dma((6,)), dma((6,)),
            dma((6, 2)), dma((6, 2)),
            dma((6,)), dma((6,)),
            dma((per_z // 3, nz)), dma((per_z // 3, nz)),
            dma((1,)), dma((1,)),
            dma((2,)),
        ],
        compiler_params=pltpu.CompilerParams(
            collective_id=0, has_side_effects=True, vmem_limit_bytes=48 * 1024 * 1024),
    )(gs, xs, ks)
    kg = ok.reshape(per_z, per_col, 128).transpose(1, 0, 2).reshape(per_col, per_z * 128)
    kg = jnp.where(c == 0, kg[:, : kernels.shape[0]], kg[:, per_z * 128 - kernels.shape[0] :])
    return om.reshape(out_cotangent.shape), oi.reshape(features.shape), kg.T


def with_halo(x, sides, width):
    for axis, dim in sides:
        size, length = (lax.axis_size(axis), x.shape[dim])
        up = [(i, (i + 1) % size) for i in range(size - 1)]
        down = [(j, i) for i, j in up]
        last = lax.slice_in_dim(x, length - width, length, axis=dim)
        initial = lax.slice_in_dim(x, 0, width, axis=dim)
        before = lax.ppermute(last, axis, up)
        after = lax.ppermute(initial, axis, down)
        x = jnp.concatenate([before, x, after], axis=dim)
    return x


def local(features, kernels, out_cotangent):
    rows_dev = features.shape[0]
    cols_dev = features.shape[1]
    chans = features.shape[2]
    outs_n = out_cotangent.shape[3]
    padding_margin = SECOND_SPACING
    x_ext = with_halo(features, (("row", 0), ("col", 1)), padding_margin)
    g_ext = with_halo(out_cotangent, (("row", 1), ("col", 2)), padding_margin)
    w_cols = lax.all_gather(kernels, "col", axis=1, tiled=True)
    w_full = lax.all_gather(w_cols, "row", axis=0, tiled=True)
    w_blocks = w_full.reshape(2, 9, chans, outs_n)
    pixels = rows_dev * cols_dev
    maps = []
    grads = []
    grad_in = jnp.zeros((pixels, chans), jnp.float32)
    for branch_index, dilation_rate in ((0, FIRST_SPACING), (1, SECOND_SPACING)):
        result = jnp.zeros((pixels, outs_n), jnp.float32)
        g_flat = out_cotangent[branch_index].reshape(pixels, outs_n)
        for kernel_tap in range(9):
            shift_down = (kernel_tap // 3 - 1) * dilation_rate
            shift_across = (kernel_tap % 3 - 1) * dilation_rate
            x_tap = x_ext[
                padding_margin + shift_down : padding_margin + shift_down + rows_dev,
                padding_margin + shift_across : padding_margin + shift_across + cols_dev,
            ].reshape(pixels, chans)
            g_tap = g_ext[
                branch_index,
                padding_margin - shift_down : padding_margin - shift_down + rows_dev,
                padding_margin - shift_across : padding_margin - shift_across + cols_dev,
            ].reshape(pixels, outs_n)
            weight = w_blocks[branch_index, kernel_tap]
            result = result + jnp.dot(x_tap, weight, preferred_element_type=jnp.float32)
            grad_in = grad_in + lax.dot_general(
                g_tap, weight, (((1,), (1,)), ((), ())), preferred_element_type=jnp.float32
            )
            grads.append(
                lax.dot_general(
                    x_tap, g_flat, (((0,), (0,)), ((), ())), preferred_element_type=jnp.float32
                )
            )
        maps.append(result.reshape(rows_dev, cols_dev, outs_n).astype(jnp.bfloat16))
    branch_maps = jnp.stack(maps, 0)
    input_grad = grad_in.reshape(rows_dev, cols_dev, chans).astype(jnp.bfloat16)
    local_grad = jnp.concatenate(grads, 0)
    total_cells = rows_dev * lax.axis_size("row") * cols_dev * lax.axis_size("col")
    scale = 1.0 / jnp.sqrt(jnp.float32(total_cells))
    partial_grad = lax.psum_scatter(local_grad, "row", scatter_dimension=0, tiled=True)
    kernel_grad = lax.psum_scatter(partial_grad, "col", scatter_dimension=1, tiled=True)
    return (branch_maps, input_grad, kernel_grad * scale)


def solution(mesh):
    n_row, n_col = mesh.shape["row"], mesh.shape["col"]
    fits = n_col == 4 and n_row == 8
    run = functools.partial(phased, n_row, n_col) if fits else local

    placed = (P("row", "col", None), P("row", "col"), P(None, "row", "col", None))
    return jax.shard_map(
        run,
        mesh=mesh,
        in_specs=placed,
        out_specs=(P(None, "row", "col", None), P("row", "col", None), P("row", "col")),
        check_vma=False,
    )
```

```python
import functools

import jax
import jax.numpy as jnp
from jax import lax
from jax.experimental import pallas as pl
from jax.experimental.pallas import tpu as pltpu
from jax.sharding import PartitionSpec as P

FIRST_SPACING = 12
SECOND_SPACING = 24
UNITS = 36
SLOT = 48
MESH = pl.DeviceIdType.MESH


def kernel(n_row, n_col, scale, gs_ref, xs_ref, ks_ref, om_ref, oi_ref, ok_ref,
           ga, xa, gp, xp, kb, k2, ru, ra, sb, rb1, rb2, tc, rc, fin, fx, macc, iacc, ms, igs,
           a_send, a_recv, h_send, h_recv, k_send, k_recv, o_send, o_recv,
           p_send, p_recv, s_send, s_recv, q_send, q_recv, z_send, z_recv, l_send, l_recv, own_sem):
    nz = n_row // 2
    per_z = UNITS // nz
    r = lax.axis_index("row")
    j = lax.axis_index("col")
    z = r // 2
    c = r % 2
    sib = r + 1 - 2 * c
    cols = [lax.rem(j + i, n_col) for i in range(1, n_col)]
    zs = [lax.rem(z + i, nz) for i in range(1, nz)]
    across = j + 1 - 2 * (j % 2)
    along = j + 2 - 4 * (j // 2)
    first = jnp.where(c == 0, across, along)
    second = jnp.where(c == 0, along, across)
    corner = first + second - j
    far = r - 1 + 2 * c
    has_up = r > 0
    has_down = r < n_row - 1
    has_far = jnp.where(c == 0, has_up, has_down)

    barrier = pltpu.get_barrier_semaphore()
    for s in cols:
        pl.semaphore_signal(barrier, inc=1, device_id={"col": s}, device_id_type=MESH)
    for zz in zs:
        pl.semaphore_signal(barrier, inc=1, device_id={"row": zz * 2 + c}, device_id_type=MESH)
    pl.semaphore_signal(barrier, inc=1, device_id={"row": sib}, device_id_type=MESH)

    @pl.when(has_far)
    def _():
        pl.semaphore_signal(barrier, inc=1, device_id={"row": far}, device_id_type=MESH)

    pl.semaphore_wait(barrier, n_col - 1 + nz - 1 + 1 + jnp.where(has_far, 1, 0))

    def remote(src, dst, ssem, rsem, dev):
        return pltpu.make_async_remote_copy(
            src_ref=src, dst_ref=dst, send_sem=ssem, recv_sem=rsem,
            device_id=dev, device_id_type=MESH)

    def deal(a, s):
        if a == 0:
            src, dst = gs_ref.at[:, :, s], ga.at[1, j]
        else:
            src, dst = xs_ref.at[:, s], xa.at[1, j]
        return remote(src, dst, a_send.at[a, s], a_recv.at[a, j], {"col": s})

    def dealt(a, s):
        if a == 0:
            src, dst = gs_ref.at[:, :, s], ga.at[1, s]
        else:
            src, dst = xs_ref.at[:, s], xa.at[1, s]
        return remote(src, dst, a_send.at[a, s], a_recv.at[a, s], {"col": s})

    sends = []

    def go(cp):
        cp.start()
        sends.append(cp)

    for s in cols:
        go(deal(0, s))
    for zz in zs:
        go(remote(ks_ref, kb.at[c, j, z], k_send.at[0, zz], k_recv.at[0, z], {"row": zz * 2 + c}))
    for s in cols:
        go(deal(1, s))
    kb[c, j, z] = ks_ref[...]
    own_g = pltpu.make_async_copy(gs_ref.at[:, :, j], ga.at[1, j], own_sem.at[0])
    own_x = pltpu.make_async_copy(xs_ref.at[:, j], xa.at[1, j], own_sem.at[1])
    own_g.start()
    own_x.start()

    def halo(a, s, up):
        buf = ga if a == 0 else xa
        to = r - 1 if up else r + 1
        d = 0 if up else 1
        return remote(buf.at[1, s], buf.at[2 if up else 0, s],
                      h_send.at[a, d, s], h_recv.at[a, d, s], {"row": to})

    def spread(a, s):
        @pl.when(has_up)
        def _():
            halo(a, s, True).start()

        @pl.when(has_down)
        def _():
            halo(a, s, False).start()

    def gather(a):
        for i in range(1, n_col):
            s = lax.rem(j + n_col - i, n_col)
            dealt(a, s).wait_recv()
            spread(a, s)

    def halo_wait(a):
        for s in range(n_col):
            @pl.when(has_down)
            def _():
                halo(a, s, True).wait_recv()

            @pl.when(has_up)
            def _():
                halo(a, s, False).wait_recv()

    def halo_done(a):
        for s in range(n_col):
            @pl.when(has_up)
            def _():
                halo(a, s, True).wait_send()

            @pl.when(has_down)
            def _():
                halo(a, s, False).wait_send()

    own_g.wait()
    spread(0, j)
    gp[...] = jnp.zeros_like(gp)
    xp[...] = jnp.zeros_like(xp)
    gather(0)
    for i in range(1, nz):
        zz = lax.rem(z + nz - i, nz)
        remote(ks_ref, kb.at[c, j, zz], k_send.at[0, zz], k_recv.at[0, zz], {"row": zz * 2 + c}).wait_recv()

    def share(n, s, to):
        return remote(kb.at[c, s], kb.at[c, s], k_send.at[1, n], k_recv.at[1, n], {"col": to})

    go(share(0, j, first))
    go(share(1, j, second))
    own_x.wait()
    spread(1, j)
    gather(1)

    def place(n):
        for s in range(n_col):
            for b in range(2):
                block = ga[n, s, b].astype(jnp.float32)
                for h in range(2):
                    part = block[:, :, 12 * h : 12 * (h + 1)].astype(jnp.bfloat16)
                    gp[b, 2 * n : 2 * n + 2, 2 + 2 * s + h, :, 0:12, :] = part

    def place_x(n):
        for s in range(n_col):
            block = xa[n, s].astype(jnp.float32)
            for h in range(2):
                part = block[:, :, 12 * h : 12 * (h + 1)].astype(jnp.bfloat16)
                xp[2 * n : 2 * n + 2, 2 + 2 * s + h, :, 0:12, :] = part

    qs = 2 * n_col
    outs_n = gp.shape[-1]
    chans = xp.shape[-1]
    pix = 2 * qs * SLOT
    half = outs_n // n_col // 2

    def g_tap(b, t):
        d = 1 + b
        sy = (t // 3 - 1) * d
        sx = (t % 3 - 1) * d
        return gp[b, pl.ds(2 - sy, 2), pl.ds(2 - sx, qs)].reshape(pix, outs_n)

    def x_tap(b, t):
        d = 1 + b
        sy = (t // 3 - 1) * d
        sx = (t % 3 - 1) * d
        return xp[pl.ds(2 + sy, 2), pl.ds(2 + sx, qs)].reshape(pix, chans)

    def span(g):
        return pl.ds(6 * g, 6)

    def pair(g):
        us = span(g)
        return remote(ru.at[us, :, 1 - c], ra.at[us], p_send.at[g], p_recv.at[g], {"row": sib})

    def step(g, k):
        us = span(g)
        return remote(sb.at[first if k == 0 else corner, us], rb1.at[k, us],
                      s_send.at[g, k], s_recv.at[g, k], {"col": first})

    def close(g):
        us = span(g)
        return remote(sb.at[second, us], rb2.at[us], q_send.at[g], q_recv.at[g], {"col": second})

    def spine(zz, k, at):
        return remote(tc.at[pl.ds(zz * per_z + 3 * k, 3)], rc.at[at, pl.ds(3 * k, 3)],
                      z_send.at[k, zz], z_recv.at[k, at], {"row": zz * 2 + c})

    def taps_grad(g):
        b = g // 3

        def body(i, carry):
            t = 3 * (g % 3) + i
            x_here = xp[pl.ds(2, 2), pl.ds(2, qs)].reshape(pix, chans)
            res = lax.dot_general(g_tap(b, t), x_here, (((0,), (0,)), ((), ())),
                                  preferred_element_type=jnp.float32)
            for h in range(2):
                ru[2 * (9 * b + t) + h] = res[:, 128 * h : 128 * (h + 1)].reshape(n_col, 2, half, 128)
            return carry

        lax.fori_loop(0, 3, body, 0)
        pair(g).start()

    def reduce_pair(g):
        us = span(g)
        pair(g).wait_recv()
        for s in range(n_col):
            sb[s, us] = ru[us, s, c] + ra[us, s]
        for k in (1, 0):
            step(g, k).start()

    def reduce_plane(g):
        us = span(g)
        step(g, 1).wait_recv()
        sb[second, us] = sb[second, us] + rb1[1, us]
        close(g).start()
        step(g, 0).wait_recv()
        sb[j, us] = sb[j, us] + rb1[0, us]

    def reduce_spine(g):
        us = span(g)
        close(g).wait_recv()
        tc[us] = sb[j, us] + rb2[us]
        for q in (2 * g, 2 * g + 1):
            @pl.when(z != 3 * q // per_z)
            def _():
                spine(3 * q // per_z, q % (per_z // 3), z).start()

    place(1)
    place_x(1)
    taps_grad(1)
    share(0, first, first).wait_recv()
    taps_grad(4)
    reduce_pair(1)
    halo_wait(0)

    @pl.when(has_up)
    def _():
        place(0)

    @pl.when(has_down)
    def _():
        place(2)

    reduce_pair(4)
    taps_grad(3)
    go(share(2, first, second))
    reduce_plane(1)
    taps_grad(5)
    reduce_pair(3)
    reduce_plane(4)
    taps_grad(0)
    reduce_pair(5)
    reduce_spine(1)
    taps_grad(2)
    reduce_pair(0)
    reduce_plane(3)
    reduce_spine(4)
    reduce_pair(2)
    reduce_plane(5)

    share(1, second, second).wait_recv()
    share(2, corner, second).wait_recv()
    swap = remote(kb.at[c], kb.at[c], k_send.at[2, 0], k_recv.at[2, 0], {"row": sib})
    go(swap)
    reduce_spine(3)
    reduce_plane(0)
    remote(kb.at[1 - c], kb.at[1 - c], k_send.at[2, 0], k_recv.at[2, 0], {"row": sib}).wait_recv()
    for u in range(UNITS):
        zz, v = divmod(u, per_z)
        mid = per_z // 2
        if v < mid:
            val = kb[0, :, zz, v]
        elif v > mid:
            val = kb[1, :, zz, v - mid]
        else:
            val = kb[0, :, zz, mid] + kb[1, :, zz, 0]
        k2[u // 2, :, 128 * (u % 2) : 128 * (u % 2 + 1)] = val.reshape(outs_n, 128)

    def pack(acc, s):
        halves = [acc[:, 2 * s + h, :, 0:12, :] for h in range(2)]
        return jnp.concatenate(halves, axis=2).astype(jnp.bfloat16)

    def back(k, s, at):
        if k == 2:
            src, dst = igs.at[s], oi_ref.at[:, at]
        else:
            src, dst = ms.at[s, k], om_ref.at[k, :, at]
        return remote(src, dst, o_send.at[k, s], o_recv.at[k, at], {"col": s})

    def input_part(b):
        def body(t, carry):
            res = jnp.dot(g_tap(b, t), k2[9 * b + t], preferred_element_type=jnp.float32)
            iacc[...] += res.reshape(iacc.shape)
            return carry

        lax.fori_loop(0, 9, body, 0)

    def map_part(b):
        macc[...] = jnp.zeros_like(macc)

        def body(t, carry):
            res = lax.dot_general(x_tap(b, t), k2[9 * b + t], (((1,), (1,)), ((), ())),
                                  preferred_element_type=jnp.float32)
            macc[...] += res.reshape(macc.shape)
            return carry

        lax.fori_loop(0, 9, body, 0)
        for s in range(n_col):
            ms[s, b] = pack(macc, s)
        for s in cols:
            back(b, s, j).start()
        om_ref[b, :, j] = ms[j, b]

    iacc[...] = jnp.zeros_like(iacc)
    input_part(0)
    reduce_plane(2)
    reduce_spine(5)
    reduce_spine(0)
    input_part(1)
    for s in range(n_col):
        igs[s] = pack(iacc, s)
    for s in cols:
        back(2, s, j).start()
    oi_ref[:, j] = igs[j]
    reduce_spine(2)

    halo_wait(1)

    @pl.when(has_up)
    def _():
        place_x(0)

    @pl.when(has_down)
    def _():
        place_x(2)

    map_part(0)
    map_part(1)
    mine = tc[pl.ds(z * per_z, per_z)]
    for i in range(1, nz):
        zz = lax.rem(z + nz - i, nz)
        for k in range(per_z // 3):
            spine(zz, k, zz).wait_recv()
        mine = mine + rc[zz]
    fin[...] = mine * scale
    last = remote(fin, fx, l_send.at[0], l_recv.at[0], {"row": sib})
    last.start()
    ok_ref[:, c] = fin[...]
    last.wait()
    ok_ref[:, 1 - c] = fx[...]

    for k in range(3):
        for i in range(1, n_col):
            s = lax.rem(j + n_col - i, n_col)
            back(k, s, s).wait_recv()
        for s in cols:
            back(k, s, j).wait_send()
    for g in range(6):
        pair(g).wait_send()
        for k in (1, 0):
            step(g, k).wait_send()
        close(g).wait_send()
    for zz in zs:
        for k in range(per_z // 3):
            spine(zz, k, z).wait_send()
    for cp in sends:
        cp.wait_send()
    halo_done(0)
    halo_done(1)


def phased(n_row, n_col, features, kernels, out_cotangent):
    nz = n_row // 2
    per_z = UNITS // nz
    rows_dev, cols_dev, chans = features.shape
    outs_n = out_cotangent.shape[3]
    kk = 12 // n_col
    per_col = outs_n // n_col
    c = lax.axis_index("row") % 2
    bf, f32 = jnp.bfloat16, jnp.float32
    xs = features.reshape(2, n_col, kk, cols_dev, chans)
    gs = out_cotangent.reshape(2, 2, n_col, kk, cols_dev, outs_n)
    kt = kernels.T
    kt = jnp.where(c == 0, jnp.pad(kt, ((0, 0), (0, 64))), jnp.pad(kt, ((0, 0), (64, 0))))
    held = (per_z + 1) // 2
    ks = kt.reshape(per_col, held, 128).transpose(1, 0, 2)
    cells = rows_dev * n_row * cols_dev * n_col
    scale = 1.0 / float(cells) ** 0.5
    qs = 2 * n_col
    half = per_col // 2
    vm = pl.BlockSpec(memory_space=pltpu.VMEM)
    dma = pltpu.SemaphoreType.DMA
    om, oi, ok = pl.pallas_call(
        functools.partial(kernel, n_row, n_col, scale),
        out_shape=(
            jax.ShapeDtypeStruct(gs.shape, bf),
            jax.ShapeDtypeStruct(xs.shape, bf),
            jax.ShapeDtypeStruct((per_z, 2, half, 128), f32),
        ),
        in_specs=[pl.BlockSpec(memory_space=pltpu.HBM)] * 2 + [vm],
        out_specs=(vm,) * 3,
        scratch_shapes=[
            pltpu.VMEM((3, n_col, 2, 2, kk, cols_dev, outs_n), bf),
            pltpu.VMEM((3, n_col, 2, kk, cols_dev, chans), bf),
            pltpu.VMEM((2, 6, qs + 4, kk, 16, outs_n), bf),
            pltpu.VMEM((6, qs + 4, kk, 16, chans), bf),
            pltpu.VMEM((2, n_col, nz, held, per_col, 128), bf),
            pltpu.VMEM((18, outs_n, chans), bf),
            pltpu.VMEM((UNITS, n_col, 2, half, 128), f32),
            pltpu.VMEM((UNITS, n_col, half, 128), f32),
            pltpu.VMEM((n_col, UNITS, half, 128), f32),
            pltpu.VMEM((2, UNITS, half, 128), f32),
            pltpu.VMEM((UNITS, half, 128), f32),
            pltpu.VMEM((UNITS, half, 128), f32),
            pltpu.VMEM((nz, per_z, half, 128), f32),
            pltpu.VMEM((per_z, half, 128), f32),
            pltpu.VMEM((per_z, half, 128), f32),
            pltpu.VMEM((2, qs, kk, 16, outs_n), f32),
            pltpu.VMEM((2, qs, kk, 16, chans), f32),
            pltpu.VMEM((n_col, 2, 2, kk, cols_dev, outs_n), bf),
            pltpu.VMEM((n_col, 2, kk, cols_dev, chans), bf),
            dma((2, n_col)), dma((2, n_col)),
            dma((2, 2, n_col)), dma((2, 2, n_col)),
            dma((3, 4)), dma((3, 4)),
            dma((3, n_col)), dma((3, n_col)),
            dma((6,)), dma((6,)),
            dma((6, 2)), dma((6, 2)),
            dma((6,)), dma((6,)),
            dma((per_z // 3, nz)), dma((per_z // 3, nz)),
            dma((1,)), dma((1,)),
            dma((2,)),
        ],
        compiler_params=pltpu.CompilerParams(
            collective_id=0, has_side_effects=True, vmem_limit_bytes=48 * 1024 * 1024),
    )(gs, xs, ks)
    kg = ok.reshape(per_z, per_col, 128).transpose(1, 0, 2).reshape(per_col, per_z * 128)
    kg = jnp.where(c == 0, kg[:, : kernels.shape[0]], kg[:, per_z * 128 - kernels.shape[0] :])
    return om.reshape(out_cotangent.shape), oi.reshape(features.shape), kg.T


def with_halo(x, sides, width):
    for axis, dim in sides:
        size, length = (lax.axis_size(axis), x.shape[dim])
        up = [(i, (i + 1) % size) for i in range(size - 1)]
        down = [(j, i) for i, j in up]
        last = lax.slice_in_dim(x, length - width, length, axis=dim)
        initial = lax.slice_in_dim(x, 0, width, axis=dim)
        before = lax.ppermute(last, axis, up)
        after = lax.ppermute(initial, axis, down)
        x = jnp.concatenate([before, x, after], axis=dim)
    return x


def local(features, kernels, out_cotangent):
    rows_dev = features.shape[0]
    cols_dev = features.shape[1]
    chans = features.shape[2]
    outs_n = out_cotangent.shape[3]
    padding_margin = SECOND_SPACING
    x_ext = with_halo(features, (("row", 0), ("col", 1)), padding_margin)
    g_ext = with_halo(out_cotangent, (("row", 1), ("col", 2)), padding_margin)
    w_cols = lax.all_gather(kernels, "col", axis=1, tiled=True)
    w_full = lax.all_gather(w_cols, "row", axis=0, tiled=True)
    w_blocks = w_full.reshape(2, 9, chans, outs_n)
    pixels = rows_dev * cols_dev
    maps = []
    grads = []
    grad_in = jnp.zeros((pixels, chans), jnp.float32)
    for branch_index, dilation_rate in ((0, FIRST_SPACING), (1, SECOND_SPACING)):
        result = jnp.zeros((pixels, outs_n), jnp.float32)
        g_flat = out_cotangent[branch_index].reshape(pixels, outs_n)
        for kernel_tap in range(9):
            shift_down = (kernel_tap // 3 - 1) * dilation_rate
            shift_across = (kernel_tap % 3 - 1) * dilation_rate
            x_tap = x_ext[
                padding_margin + shift_down : padding_margin + shift_down + rows_dev,
                padding_margin + shift_across : padding_margin + shift_across + cols_dev,
            ].reshape(pixels, chans)
            g_tap = g_ext[
                branch_index,
                padding_margin - shift_down : padding_margin - shift_down + rows_dev,
                padding_margin - shift_across : padding_margin - shift_across + cols_dev,
            ].reshape(pixels, outs_n)
            weight = w_blocks[branch_index, kernel_tap]
            result = result + jnp.dot(x_tap, weight, preferred_element_type=jnp.float32)
            grad_in = grad_in + lax.dot_general(
                g_tap, weight, (((1,), (1,)), ((), ())), preferred_element_type=jnp.float32
            )
            grads.append(
                lax.dot_general(
                    x_tap, g_flat, (((0,), (0,)), ((), ())), preferred_element_type=jnp.float32
                )
            )
        maps.append(result.reshape(rows_dev, cols_dev, outs_n).astype(jnp.bfloat16))
    branch_maps = jnp.stack(maps, 0)
    input_grad = grad_in.reshape(rows_dev, cols_dev, chans).astype(jnp.bfloat16)
    local_grad = jnp.concatenate(grads, 0)
    total_cells = rows_dev * lax.axis_size("row") * cols_dev * lax.axis_size("col")
    scale = 1.0 / jnp.sqrt(jnp.float32(total_cells))
    partial_grad = lax.psum_scatter(local_grad, "row", scatter_dimension=0, tiled=True)
    kernel_grad = lax.psum_scatter(partial_grad, "col", scatter_dimension=1, tiled=True)
    return (branch_maps, input_grad, kernel_grad * scale)


def solution(mesh):
    n_row, n_col = mesh.shape["row"], mesh.shape["col"]
    fits = n_col == 4 and n_row == 8
    run = functools.partial(phased, n_row, n_col) if fits else local

    placed = (P("row", "col", None), P("row", "col"), P(None, "row", "col", None))
    return jax.shard_map(
        run,
        mesh=mesh,
        in_specs=placed,
        out_specs=(P(None, "row", "col", None), P("row", "col", None), P("row", "col")),
        check_vma=False,
    )
```
